128 devices in a mesh: mesh: 32 (over x, y_lo, z), chaos: 4 (over y_hi, core).
Axes of the slice: x: 4, y: 4 (y_hi: 2, y_lo: 2; y = y_hi * 2 + y_lo), z: 4, core: 2. Of those that a mesh axis runs over, the one named last changes fastest.
Arguments:
- field_coeffs: bfloat16 [120, 3, 131072], P('chaos', None, 'mesh'), may hold values from -6 to 6
- face_list: int32 [32, 2, 512], P('mesh'), may hold values from 0 to 4095
- face_count: int32 [32, 2], P('mesh'), may hold values from 128 to 512, as said below
- neighbors: int32 [8, 131072], P(None, 'mesh'), may hold values from 0 to 5119
- diag_modes: float32 [9, 131072], P(None, 'mesh'), may hold values from 1 to 10
- coupling: float32 [9, 8, 131072], P(None, None, 'mesh'), may hold values from 0.2 to 2
- triple: bfloat16 [9, 120, 120], replicated, may hold values from -0.0390625 to 0.0390625
Outputs:
- applied: float32 [120, 3, 131072], P('chaos', None, 'mesh')
The draws below stay inside these ranges and needn't reach their ends.
Inputs may be any that keep to these rules, and one draw needn't show every extreme that they name: face_count equals 512 for at least one list in every draw.
All inputs are finite; a program needn't handle non-finite values.
Results may differ from the reference program's by a relative error of at most 0.0003.
Values may be sent and summed in bfloat16 or wider, within the bound.
A program may use at most 640 MiB of HBM per device.

```python
import math
import jax
import jax.numpy as jnp
from jax import lax

P_SIZE = 120
K1 = 9
S = 8
F = 512
NODE_DEV = 4096
E = 5120
NODES = 131072
N_MESH = 32


def draw_face_count(key, part):
    key = jax.random.fold_in(key, 7)
    first_key, second_key = jax.random.split(key)
    counts = jax.random.randint(first_key, (2 * N_MESH,), F // 4, F + 1)
    filled = jax.random.randint(second_key, (), 0, 2 * N_MESH)
    counts = jnp.where(jnp.arange(2 * N_MESH) == filled, F, counts)
    return counts.reshape(N_MESH, 2).astype(jnp.int32)


def touch_ends(values, rng, least, largest):
    index_at = [jax.random.randint(jax.random.fold_in(rng, axis), (), 0, length) for axis, length in enumerate(values.shape)]
    widest = values.shape.index(max(values.shape))
    next_to = index_at[:widest] + [(index_at[widest] + 1) % values.shape[widest]] + index_at[widest + 1:]
    return values.at[tuple(index_at)].set(least).at[tuple(next_to)].set(largest)


def steps_of(own_key, extent, shards, low, high):
    gain = 1.0
    for axis_at, blocks in shards:
        draws = jax.random.uniform(jax.random.fold_in(jax.random.fold_in(own_key, 6), axis_at), (blocks,), jnp.float32, low / len(shards), high / len(shards))
        gain = gain * jnp.repeat(jnp.exp(draws), extent[axis_at] // blocks).reshape((-1,) + (1,) * (len(extent) - 1 - axis_at))
    return gain


def noise(rng, extent, deviation, most, cuts=(), held_as=jnp.bfloat16):
    drawn = deviation * jax.random.normal(rng, extent, jnp.float32)
    if cuts:
        drawn = drawn * steps_of(rng, extent, cuts, -0.22, 0.18)
    return jnp.clip(drawn, -most, most).astype(held_as)


def setup_inputs(seed: int = 0) -> dict:
    arg_keys = jax.random.split(jax.random.key(seed), 8)
    field_coeffs = noise(arg_keys[0], (P_SIZE, 3, NODES), 1.0, 6.0, ((0, 4), (2, 32)))
    face_list = touch_ends(jax.random.randint(arg_keys[1], (N_MESH, 2, F), 0, NODE_DEV), jax.random.fold_in(arg_keys[1], 1), 0, NODE_DEV - 1).astype(jnp.int32)
    face_count = draw_face_count(jax.random.fold_in(arg_keys[7], 71), 0)
    neighbors = touch_ends(jax.random.randint(arg_keys[3], (S, NODES), 0, E), jax.random.fold_in(arg_keys[3], 1), 0, E - 1).astype(jnp.int32)
    diag_modes = jnp.clip(jnp.exp(math.log(10.0) - 2.3025851 * jax.random.uniform(arg_keys[4], (K1, NODES), jnp.float32) ** steps_of(arg_keys[4], (K1, NODES), ((1, 32),), -0.2, 0.2)), 1.0, 10.0)
    coupling = jnp.clip(jnp.exp(math.log(2.0) - 2.3025851 * jax.random.uniform(arg_keys[5], (K1, S, NODES), jnp.float32) ** steps_of(arg_keys[5], (K1, S, NODES), ((2, 32),), -0.2, 0.2)), 0.2, 2.0)
    triple = noise(arg_keys[6], (K1, P_SIZE, P_SIZE), (P_SIZE * K1 * 25) ** -0.5, 0.0390625)
    return dict(field_coeffs=field_coeffs, face_list=face_list, face_count=face_count, neighbors=neighbors, diag_modes=diag_modes, coupling=coupling, triple=triple)


def field_terms(wide, neighbors_m, diag_m, coupling_m):
    total = diag_m[:, None, :] * wide[:, :, :NODE_DEV]
    for slot_index in range(S):
        taken = jnp.take(wide, neighbors_m[slot_index], axis=2)
        total = total - coupling_m[:, slot_index][:, None, :] * taken
    return total


def reference(field_coeffs, face_list, face_count, neighbors, diag_modes, coupling, triple):
    blocks = field_coeffs.reshape(P_SIZE, 3, N_MESH, NODE_DEV)
    face_rows = jax.vmap(lambda block, index: block[:, :, index], in_axes=(2, 0))(blocks, face_list)
    keep = (jnp.arange(F, dtype=jnp.int32)[None, None, :] < face_count[:, :, None]).astype(jnp.bfloat16)
    face_rows = face_rows * keep[:, None, None, :, :]
    zeros_face = jnp.zeros((1, P_SIZE, 3, F), jnp.bfloat16)
    from_lower = jnp.concatenate([zeros_face, face_rows[:-1, :, :, 1, :]], axis=0)
    from_upper = jnp.concatenate([face_rows[1:, :, :, 0, :], zeros_face], axis=0)
    local_rows = jnp.moveaxis(blocks, 2, 0)
    nbr_parts = jnp.moveaxis(neighbors.reshape(S, N_MESH, NODE_DEV), 1, 0)
    diag_parts = jnp.moveaxis(diag_modes.reshape(K1, N_MESH, NODE_DEV), 1, 0)
    coup_parts = jnp.moveaxis(coupling.reshape(K1, S, N_MESH, NODE_DEV), 2, 0)
    triple_wide = triple.astype(jnp.float32)

    def one_part(items):
        local_m, lower_m, upper_m, nbr_m, diag_m, coup_m = items
        extended = jnp.concatenate([local_m, lower_m, upper_m], axis=2).astype(jnp.float32)
        flat = extended.reshape(1, P_SIZE * 3, E)
        terms = field_terms(flat, nbr_m, diag_m, coup_m).reshape(K1, P_SIZE, 3 * NODE_DEV)
        result = jnp.einsum('kij,kjx->ix', triple_wide, terms, precision=lax.Precision.HIGHEST)
        return result.reshape(P_SIZE, 3, NODE_DEV)

    parts_out = lax.map(one_part, (local_rows, from_lower, from_upper, nbr_parts, diag_parts, coup_parts))
    return jnp.moveaxis(parts_out, 0, 2).reshape(P_SIZE, 3, NODES)
```

```python
import jax
import jax.numpy as jnp
from jax import lax
from jax.experimental import pallas as pl
from jax.experimental.pallas import tpu as pltpu
from jax.sharding import PartitionSpec as P
BF=jnp.bfloat16; F32=jnp.float32
NT=16
def iota(shape,d): return lax.broadcasted_iota(jnp.int32, shape, d)
def chaos_of(y,c,q):
    yy = jnp.where(q>=2, 1-y, y); cc = jnp.where(q%2==1, 1-c, c)
    return 2*yy+cc
def prep_triple(tri_ref, tt_ref, y, c):
    r=iota((128,120),0); i=iota((128,120),1)
    q=r//32; rr=r%32
    d=2*jnp.where(q>=2,1-y,y)+jnp.where(q%2==1,1-c,c)
    sel_l=jnp.where((rr<30)&(i==d*30+rr),1.0,0.0).astype(BF)
    j=iota((120,128),0); a=iota((120,128),1)
    for k in range(9):
        tl=jnp.dot(sel_l,tri_ref[k],preferred_element_type=F32).astype(BF)
        off=64*(k%2)
        b=a-off; h=b//32; bb=b%32
        dj=2*y+jnp.where(h==1,1-c,c)
        sel_r=jnp.where((b>=0)&(b<64)&(bb<30)&(j==dj*30+bb),1.0,0.0).astype(BF)
        t=jnp.dot(tl,sel_r,preferred_element_type=F32)
        if k%2==0: keep=t
        if k%2==1: tt_ref[:, (k-1)*64:(k+1)*64]=(keep+t).astype(BF)
    tt_ref[:, 512:640]=keep.astype(BF)
def build_table(xs, tab, nb0, nb1):
    def body(b,_):
        lanes=pl.ds(pl.multiple_of(b*128,128),128)
        for h in range(2):
            z2=jnp.zeros((2,128),F32)
            parts=[]
            for cc in range(3):
                parts += [xs[h][cc,:,lanes].astype(F32), z2]
            parts.append(jnp.zeros((32,128),F32))
            v=jnp.concatenate(parts,axis=0)
            tab[pl.ds(256*b+h,128,stride=2),:]=v.T
        return 0
    lax.fori_loop(nb0,nb1,body,0)
def gather_tile(idx_ref, tab, stage, t, slots):
    for s in slots:
        for u0 in range(0,128,16):
            ii=[idx_ref[t,s,u0+u] for u in range(16)]
            vs=[tab[pl.ds(pl.multiple_of(i,2),2),:] for i in ii]
            for u in range(16):
                stage[pl.ds((s*128+u0+u)*2,2),:]=vs[u]
def expand(sel_ref, stage, tab, gt, t, n0):
    for s in range(9):
        if s<8: w=[stage[pl.ds(s*256+h,128,stride=2),:] for h in range(2)]
        else: w=[tab[pl.ds(2*n0+h,128,stride=2),:] for h in range(2)]
        wn=jnp.concatenate(w,axis=1).astype(BF)
        gt[s]=lax.dot_general(sel_ref[...],wn,(((1,),(1,)),((),())),preferred_element_type=F32)
def combine(gt, coup, diag, ax, lanes, cc, h, jh):
    rows=pl.ds(pl.multiple_of(h*96+cc*32+jh*16,16),16)
    g=[gt[s,rows,:] for s in range(9)]
    for k in range(9):
        acc=diag[k:k+1,lanes]*g[8]
        for s in range(8):
            acc=acc-coup[k,s:s+1,lanes]*g[s]
        hi=acc.astype(BF)
        lo=(acc-hi.astype(F32)).astype(BF)
        ro=pl.ds(pl.multiple_of(k*64+h*32+jh*16,16),16)
        ax[cc,ro,0:128]=hi
        ax[cc,ro,128:256]=lo
def k2(sc, xo, xp, idx_ref, coup, diag, tri, loc, snd, tab, stage, gt, ax, tt, sel):
    y=sc[0]; c=sc[1]
    prep_triple(tri,tt,y,c)
    r=iota((192,256),0); kk=iota((192,256),1)
    sel[...]=jnp.where(kk==jnp.where(r>=96,r+32,r),1.0,0.0).astype(BF)
    build_table([xo,xp],tab,0,40)
    def tile(t,_):
        lanes=pl.ds(pl.multiple_of(t*128,128),128)
        n0=c*2048+t*128
        gather_tile(idx_ref,tab,stage,t,range(8))
        expand(sel,stage,tab,gt,t,n0)
        def cb(q,_):
            for cc in range(3): combine(gt,coup,diag,ax,lanes,cc,q//2,q%2)
            return 0
        lax.fori_loop(0,4,cb,0)
        for cc in range(3):
            o=jnp.dot(tt[:,0:576],ax[cc],preferred_element_type=F32)
            o=o[:,0:128]+o[:,128:256]
            loc[cc,:,lanes]=o[0:64]
            snd[cc,:,lanes]=o[64:128]
        return 0
    lax.fori_loop(0,NT,tile,0)
def call_k2(sc,xo,xp,idx,coup,diag,tri,kern=k2):
    gs=pltpu.PrefetchScalarGridSpec(num_scalar_prefetch=1,grid=(1,),
      in_specs=[pl.BlockSpec((3,30,5120),lambda i,s:(0,0,0)),pl.BlockSpec((3,30,5120),lambda i,s:(0,0,0)),
        pl.BlockSpec((16,8,128),lambda i,s:(s[1],0,0),memory_space=pltpu.SMEM),
        pl.BlockSpec((9,8,2048),lambda i,s:(0,0,s[1])),pl.BlockSpec((9,2048),lambda i,s:(0,s[1])),
        pl.BlockSpec((9,120,120),lambda i,s:(0,0,0))],
      out_specs=[pl.BlockSpec((3,64,2048),lambda i,s:(0,0,0)),pl.BlockSpec((3,64,2048),lambda i,s:(0,0,0))],
      scratch_shapes=[pltpu.VMEM((10240,128),F32),pltpu.VMEM((2048,128),F32),pltpu.VMEM((9,192,128),F32),
        pltpu.VMEM((3,576,256),BF),pltpu.VMEM((128,640),BF),pltpu.VMEM((192,256),BF)])
    return pl.pallas_call(kern,grid_spec=gs,out_shape=[jax.ShapeDtypeStruct((3,64,2048),F32)]*2,
      compiler_params=pltpu.CompilerParams(vmem_limit_bytes=60<<20))(sc,xo,xp,idx,coup,diag,tri)

def face_kernel(x,fl,fc,o):
    def body(b,acc):
        m=iota((512,1024),0)+b*512
        oh=jnp.where(m==fl[...],1.0,0.0).astype(BF)
        lanes=pl.ds(pl.multiple_of(b*512,512),512)
        return tuple(acc[cc]+jnp.dot(x[cc,:,lanes],oh,preferred_element_type=F32) for cc in range(3))
    acc=lax.fori_loop(0,8,body,tuple(jnp.zeros((30,1024),F32) for _ in range(3)))
    l=iota((1,1024),1)
    keep=jnp.where(l%512<jnp.where(l<512,fc[0,0],fc[0,1]),1.0,0.0)
    for cc in range(3):
        o[cc]=(acc[cc]*keep).astype(BF)
def call_faces(x,fl,fc):
    return pl.pallas_call(face_kernel,out_shape=jax.ShapeDtypeStruct((3,30,1024),BF),
        in_specs=[pl.BlockSpec(memory_space=pltpu.VMEM)]*2+[pl.BlockSpec(memory_space=pltpu.SMEM)],
        out_specs=pl.BlockSpec(memory_space=pltpu.VMEM),
        compiler_params=pltpu.CompilerParams(vmem_limit_bytes=60<<20))(x,fl,fc)
def on_device(field_coeffs, face_list, face_count, neighbors, diag_modes, coupling, triple):
    ch=lax.axis_index("chaos"); y=ch//2; c=ch%2
    x=jnp.transpose(field_coeffs,(1,0,2))
    core=[(0,1),(1,0),(2,3),(3,2)]
    across=[(0,2),(2,0),(1,3),(3,1)]
    faces=call_faces(x,face_list.reshape(1,1024),face_count)
    n=lax.axis_size("mesh")
    lower=lax.ppermute(faces[:,:,512:],"mesh",[(s,s+1) for s in range(n-1)])
    upper=lax.ppermute(faces[:,:,:512],"mesh",[(s,s-1) for s in range(1,n)])
    xo=jnp.concatenate([x,lower,upper],axis=2)
    xp=lax.ppermute(xo,"chaos",core)
    idx=(neighbors*2).reshape(8,32,128).transpose(1,0,2)
    sc=jnp.stack([y,c]).astype(jnp.int32)
    loc,snd=call_k2(sc,xo,xp,idx,coupling,diag_modes,triple)
    f=loc+lax.ppermute(snd,"chaos",across)
    got=lax.ppermute(f[:,32:62],"chaos",core)
    own=f[:,0:30]
    out=jnp.where(c==0,jnp.concatenate([own,got],axis=2),jnp.concatenate([got,own],axis=2))
    return jnp.transpose(out,(1,0,2))
def solution(mesh):
    in_specs=(P("chaos",None,"mesh"),P("mesh",None,None),P("mesh",None),P(None,"mesh"),P(None,"mesh"),P(None,None,"mesh"),P())
    return jax.shard_map(on_device,mesh=mesh,in_specs=in_specs,out_specs=P("chaos",None,"mesh"),check_vma=False)
```

```python
import jax
import jax.numpy as jnp
from jax import lax
from jax.experimental import pallas as pl
from jax.experimental.pallas import tpu as pltpu
from jax.sharding import PartitionSpec as P
BF=jnp.bfloat16; F32=jnp.float32
NT=16
def iota(shape,d): return lax.broadcasted_iota(jnp.int32, shape, d)
def chaos_of(y,c,q):
    yy = jnp.where(q>=2, 1-y, y); cc = jnp.where(q%2==1, 1-c, c)
    return 2*yy+cc
def prep_triple(tri_ref, tt_ref, y, c):
    r=iota((128,120),0); i=iota((128,120),1)
    q=r//32; rr=r%32
    d=2*jnp.where(q>=2,1-y,y)+jnp.where(q%2==1,1-c,c)
    sel_l=jnp.where((rr<30)&(i==d*30+rr),1.0,0.0).astype(BF)
    j=iota((120,128),0); a=iota((120,128),1)
    for k in range(9):
        tl=jnp.dot(sel_l,tri_ref[k],preferred_element_type=F32).astype(BF)
        off=64*(k%2)
        b=a-off; h=b//32; bb=b%32
        dj=2*y+jnp.where(h==1,1-c,c)
        sel_r=jnp.where((b>=0)&(b<64)&(bb<30)&(j==dj*30+bb),1.0,0.0).astype(BF)
        t=jnp.dot(tl,sel_r,preferred_element_type=F32)
        if k%2==0: keep=t
        if k%2==1: tt_ref[:, (k-1)*64:(k+1)*64]=(keep+t).astype(BF)
    tt_ref[:, 512:640]=keep.astype(BF)
def gather_slots(idx_ref, tab, stage, t, s0, ns):
    for s in range(ns):
        for u0 in range(0,128,16):
            ii=[idx_ref[t,s0+s,u0+u] for u in range(16)]
            vs=[tab[i] for i in ii]
            for u in range(16):
                stage[pl.ds(pl.multiple_of((s0+s)*256,256)+(u0+u)*2,2),:]=vs[u]
def expand(sel_ref, stage, tab, gt, n0):
    def rows(s):
        if s<8: w=[stage[pl.ds(s*256+h,128,stride=2),:] for h in range(2)]
        else: w=[tab[pl.ds(n0,128),h,:] for h in range(2)]
        return jnp.concatenate(w,axis=1).astype(BF)
    for p in range(5):
        ss=[2*p,2*p+1] if p<4 else [8]
        wn=jnp.concatenate([rows(s) for s in ss],axis=0)
        r=lax.dot_general(sel_ref[...],wn,(((1,),(1,)),((),())),preferred_element_type=F32)
        for e,s in enumerate(ss): gt[s]=r[:,e*128:(e+1)*128]
def combine(gt, coup, diag, ax, lanes, cc, h, jh):
    rows=pl.ds(pl.multiple_of(h*96+cc*32+jh*16,16),16)
    g=[gt[s,rows,:] for s in range(9)]
    for k in range(9):
        acc=diag[k:k+1,lanes]*g[8]
        for s in range(8):
            acc=acc-coup[k,s:s+1,lanes]*g[s]
        hi=acc.astype(BF)
        lo=(acc-hi.astype(F32)).astype(BF)
        ro=pl.ds(pl.multiple_of(k*64+h*32+jh*16,16),16)
        ax[cc,ro,0:128]=hi
        ax[cc,ro,128:256]=lo

MESH=pl.DeviceIdType.MESH
LAG=4

def build_table(x, tab, h):
    def body(b,_):
        lanes=pl.ds(pl.multiple_of(b*128,128),128)
        z2=jnp.zeros((2,128),F32)
        parts=[]
        for cc in range(3):
            parts += [x[cc,:,lanes].astype(F32), z2]
        parts.append(jnp.zeros((32,128),F32))
        v=jnp.concatenate(parts,axis=0)
        tab[pl.ds(pl.multiple_of(128*b,128),128),h,:]=v.T
        return 0
    lax.fori_loop(0,32,body,0)

def gather_faces(fl, fc, tab, fbuf, fsend):
    for side in range(2):
        def body(b,_):
            vs=[tab[fl[side,b*32+u]] for u in range(32)]
            for u in range(32): fbuf[pl.ds(2*(b*32+u),2),:]=vs[u]
            return 0
        lax.fori_loop(0,16,body,0)
        keep=iota((512,128),0)<fc[0,side]
        fsend[side]=jnp.where(keep,fbuf[pl.ds(0,512,stride=2),:],0.0).astype(BF)

def quantise(o):
    top=jnp.max(jnp.abs(o),axis=0,keepdims=True)
    inv=jnp.where(top>1e-30,32767.0/jnp.maximum(top,1e-30),0.0)
    return jnp.round(o*inv).astype(jnp.int32).astype(jnp.int16), top*(1.0/32767.0)

def kernel(x_any, fl, fc, nb_any, diag_any, coup_any, tri, out,
           tab, stage, gt, ax, tt, sel, xo, xp, nb, idx, coup, diag, fbuf, fsend, ghost,
           loc, snd, scl, rcv, rsc, psend, outv,
           lsem, xsem, fsem_s, fsem_r, qs, qr, ss, sr, ps, pr):
    ch=lax.axis_index("chaos"); m=lax.axis_index("mesh")
    y=ch//2; c=ch%2
    up=lax.rem(m+1,32); dn=lax.rem(m+31,32)
    peer={"chaos":2*y+1-c}; across={"chaos":2*(1-y)+c}
    near=[{"mesh":up,"chaos":ch},{"mesh":up,"chaos":2*y+1-c},{"mesh":dn,"chaos":ch},{"mesh":dn,"chaos":2*y+1-c}]
    half=pl.multiple_of(c*2048,2048)
    loads=[pltpu.make_async_copy(x_any,xo,lsem.at[0]),
           pltpu.make_async_copy(nb_any.at[:,pl.ds(half,2048)],nb,lsem.at[1]),
           pltpu.make_async_copy(diag_any.at[:,pl.ds(half,2048)],diag,lsem.at[2]),
           pltpu.make_async_copy(coup_any.at[:,:,pl.ds(half,2048)],coup,lsem.at[3])]
    for l in loads: l.start()
    bar=pltpu.get_barrier_semaphore()
    for d in near+[peer,across]:
        pl.semaphore_signal(bar,inc=1,device_id=d,device_id_type=MESH)
    pl.semaphore_wait(bar,6)
    xcopy=pltpu.make_async_remote_copy(src_ref=x_any,dst_ref=xp,send_sem=xsem.at[0],recv_sem=xsem.at[1],device_id=peer,device_id_type=MESH)
    xcopy.start()
    loads[0].wait()
    build_table(xo,tab,0)
    gather_faces(fl,fc,tab,fbuf,fsend)
    fcopies=[]
    for e,d in enumerate(near):
        side=1 if e<2 else 0
        f=pltpu.make_async_remote_copy(src_ref=fsend.at[side],dst_ref=ghost.at[e],send_sem=fsem_s.at[e],recv_sem=fsem_r.at[e],device_id=d,device_id_type=MESH)
        f.start(); fcopies.append(f)
    loads[1].wait()
    icopies=[pltpu.make_async_copy(nb.at[:,pl.ds(t*128,128)],idx.at[t],lsem.at[4+t]) for t in range(NT)]
    for i in icopies: i.start()
    prep_triple(tri,tt,y,c)
    r=iota((192,256),0); kk=iota((192,256),1)
    sel[...]=jnp.where(kk==jnp.where(r>=96,r+32,r),1.0,0.0).astype(BF)
    for cc in range(3): ax[cc]=jnp.zeros((576,256),BF)
    xcopy.wait()
    build_table(xp,tab,1)
    for i in icopies: i.wait()
    loads[2].wait(); loads[3].wait()
    for f in fcopies: f.wait()
    low=jnp.where(m>0,1.0,0.0); high=jnp.where(m<31,1.0,0.0)
    for e in range(4):
        tab[pl.ds(4096+(e//2)*512,512),e%2,:]=ghost[e].astype(F32)*(low if e<2 else high)

    def qcopy(t):
        return (pltpu.make_async_remote_copy(src_ref=snd.at[t],dst_ref=rcv.at[t],send_sem=qs.at[t],recv_sem=qr.at[t],device_id=across,device_id_type=MESH),
                pltpu.make_async_remote_copy(src_ref=scl.at[t],dst_ref=rsc.at[t],send_sem=ss.at[t],recv_sem=sr.at[t],device_id=across,device_id_type=MESH))
    def pcopy(t):
        lanes=pl.ds(pl.multiple_of(half+t*128,128),128)
        return pltpu.make_async_remote_copy(src_ref=psend.at[t],dst_ref=outv.at[:,:,lanes],send_sem=ps.at[t],recv_sem=pr.at[t],device_id=peer,device_id_type=MESH)
    def tmat(t):
        for cc in range(3):
            o=jnp.dot(tt[:,0:576],ax[cc],preferred_element_type=F32)
            o=o[:,0:128]+o[:,128:256]
            loc[t,cc]=o[0:64]
            q,s=quantise(o[64:128])
            snd[t,cc]=q
            scl[t,cc:cc+1,:]=s
    def finish(t):
        for q in qcopy(t): q.wait()
        lanes=pl.ds(pl.multiple_of(half+t*128,128),128)
        for cc in range(3):
            f=loc[t,cc]+rcv[t,cc].astype(jnp.int32).astype(F32)*rsc[t,cc:cc+1,:]
            outv[cc,:,lanes]=f[0:30]
            psend[t,cc]=f[32:62]
        pcopy(t).start()
    def g0(s,_):
        gather_slots(idx,tab,stage,0,s,1); return 0
    lax.fori_loop(0,8,g0,0)
    def tile(t,_):
        lanes=pl.ds(pl.multiple_of(t*128,128),128)
        n0=half+t*128
        tn=jnp.minimum(t+1,NT-1)
        expand(sel,stage,tab,gt,n0)
        @pl.when(t>0)
        def _():
            tmat(t-1)
            for q in qcopy(t-1): q.start()
        def cb(q,_):
            gather_slots(idx,tab,stage,tn,2*q,2)
            for cc in range(3): combine(gt,coup,diag,ax,lanes,cc,q//2,q%2)
            return 0
        lax.fori_loop(0,4,cb,0)
        @pl.when(t>=LAG)
        def _(): finish(t-LAG)
        return 0
    lax.fori_loop(0,NT,tile,0)
    tmat(NT-1)
    for q in qcopy(NT-1): q.start()
    for t in range(NT-LAG,NT): finish(t)
    for t in range(NT): pcopy(t).wait()
    ocopy=pltpu.make_async_copy(outv,out,lsem.at[0])
    ocopy.start(); ocopy.wait()

def call(x,fl,fc,nb,diag,coup,tri):
    V=pltpu.VMEM; D=pltpu.SemaphoreType.DMA
    anyspec=pl.BlockSpec(memory_space=pl.ANY); sm=pl.BlockSpec(memory_space=pltpu.SMEM); vm=pl.BlockSpec(memory_space=pltpu.VMEM)
    return pl.pallas_call(kernel,out_shape=jax.ShapeDtypeStruct((3,30,4096),F32),
        in_specs=[anyspec,sm,sm,anyspec,anyspec,anyspec,vm],out_specs=anyspec,
        scratch_shapes=[V((5120,2,128),F32),V((2048,128),F32),V((9,192,128),F32),V((3,576,256),BF),V((128,640),BF),V((192,256),BF),
            V((3,30,4096),BF),V((3,30,4096),BF),V((8,2048),jnp.int32),pltpu.SMEM((NT,8,128),jnp.int32),V((9,8,2048),F32),V((9,2048),F32),
            V((1024,128),F32),V((2,512,128),BF),V((4,512,128),BF),
            V((NT,3,64,128),F32),V((NT,3,64,128),jnp.int16),V((NT,8,128),F32),V((NT,3,64,128),jnp.int16),V((NT,8,128),F32),V((NT,3,30,128),F32),V((3,30,4096),F32),
            D((4+NT,)),D((2,)),D((4,)),D((4,)),D((NT,)),D((NT,)),D((NT,)),D((NT,)),D((NT,)),D((NT,))],
        compiler_params=pltpu.CompilerParams(vmem_limit_bytes=56<<20,collective_id=0,has_side_effects=True))(x,fl,fc,nb,diag,coup,tri)

def on_device(field_coeffs, face_list, face_count, neighbors, diag_modes, coupling, triple):
    x=jnp.transpose(field_coeffs,(1,0,2))
    out=call(x,face_list.reshape(2,512),face_count,neighbors,diag_modes,coupling,triple)
    return jnp.transpose(out,(1,0,2))

def solution(mesh):
    in_specs=(P("chaos",None,"mesh"),P("mesh",None,None),P("mesh",None),P(None,"mesh"),P(None,"mesh"),P(None,None,"mesh"),P())
    return jax.shard_map(on_device,mesh=mesh,in_specs=in_specs,out_specs=P("chaos",None,"mesh"),check_vma=False)
```

```python
import functools
import jax
import jax.numpy as jnp
from jax import lax
from jax.experimental import pallas as pl
from jax.experimental.pallas import tpu as pltpu
from jax.sharding import PartitionSpec as P
BF=jnp.bfloat16; F32=jnp.float32
NT=16
def iota(shape,d): return lax.broadcasted_iota(jnp.int32, shape, d)
def chaos_of(y,c,q):
    yy = jnp.where(q>=2, 1-y, y); cc = jnp.where(q%2==1, 1-c, c)
    return 2*yy+cc
def prep_triple(tri_ref, tt_ref, y, c):
    r=iota((128,120),0); i=iota((128,120),1)
    far=r>=64; w=jnp.where(far,r-64,r)
    other=w>=30; rr=jnp.where(other,w-30,w)
    d=2*jnp.where(far,1-y,y)+jnp.where(other,1-c,c)
    sel_l=jnp.where((rr<30)&(i==d*30+rr),1.0,0.0).astype(BF)
    j=iota((120,128),0); a=iota((120,128),1)
    for k in range(9):
        tl=jnp.dot(sel_l,tri_ref[k],preferred_element_type=F32).astype(BF)
        off=64*(k%2)
        b=a-off; h=b//32; bb=b%32
        dj=2*y+jnp.where(h==1,1-c,c)
        sel_r=jnp.where((b>=0)&(b<64)&(bb<30)&(j==dj*30+bb),1.0,0.0).astype(BF)
        t=jnp.dot(tl,sel_r,preferred_element_type=F32)
        if k%2==0: keep=t
        if k%2==1: tt_ref[:, (k-1)*64:(k+1)*64]=(keep+t).astype(BF)
    tt_ref[:, 512:640]=keep.astype(BF)
def gather_group(idx, tab, stage, g):
    s,u0=g//8,(g%8)*16
    vs=[tab[pl.ds(idx[s,u0+u],2),:] for u in range(16)]
    for u in range(16):
        stage[pl.ds((s*128+u0+u)*2,2),:]=vs[u]

def expand_pair(sel_ref, stage, gt, p):
    rows=[jnp.concatenate([stage[pl.ds(s*256+h,128,stride=2),:] for h in range(2)],axis=1).astype(BF) for s in (2*p,2*p+1)]
    r=lax.dot_general(sel_ref[...],jnp.concatenate(rows,axis=0),(((1,),(1,)),((),())),preferred_element_type=F32)
    for e in range(2): gt[2*p+e]=r[:,e*128:(e+1)*128]

def own_rows(xs, gt, lanes, h, cc):
    gt[8,h*96+cc*32:h*96+cc*32+30,:]=xs[h][cc,:,lanes].astype(F32)

def combine(gt, coup, diag, ax, at, q, cc, k):
    h,jh=q//2,q%2
    r0=h*96+cc*32+jh*16
    acc=diag[k:k+1,at]*gt[8,r0:r0+16,:]
    for s in range(8):
        acc=acc-coup[k,s:s+1,at]*gt[s,r0:r0+16,:]
    hi=acc.astype(BF)
    lo=(acc-hi.astype(F32)).astype(BF)
    ro=k*64+h*32+jh*16
    ax[cc,ro:ro+16,0:128]=hi
    ax[cc,ro:ro+16,128:256]=lo

def interleave(streams):
    ops=[]
    for n,st in enumerate(streams):
        for e,f in enumerate(st): ops.append(((e+0.5)/len(st),n,f))
    for _,_,f in sorted(ops,key=lambda o:o[:2]): f()

MESH=pl.DeviceIdType.MESH
LAG=4

def build_table(x, tab, h):
    def body(b,_):
        lanes=pl.ds(pl.multiple_of(b*128,128),128)
        z2=jnp.zeros((2,128),F32)
        parts=[]
        for cc in range(3):
            parts += [x[cc,:,lanes].astype(F32), z2]
        parts.append(jnp.zeros((32,128),F32))
        v=jnp.concatenate(parts,axis=0)
        tab[pl.ds(256*b+h,128,stride=2),:]=v.T
        return 0
    lax.fori_loop(0,32,body,0)

def gather_faces(fl, fc, tab, fbuf, fsend):
    for side in range(2):
        for b in range(32):
            vs=[tab[pl.ds(fl[side*4+b//8,(b%8)*16+u]*2,1),:] for u in range(16)]
            for u in range(16): fbuf[pl.ds(b*16+u,1),:]=vs[u]
        keep=iota((512,128),0)<fc[0,side]
        fsend[side]=jnp.where(keep,fbuf[...],0.0).astype(BF)

def quantise(o):
    top=jnp.maximum(jnp.max(jnp.abs(o),axis=0,keepdims=True),1e-30)
    e=jnp.ceil(64.0*jnp.log2(top*(1.0/32760.0)))
    q=jnp.clip(jnp.round(o*jnp.exp2(e*(-1.0/64.0))),-32767.0,32767.0)
    q=jnp.where(iota((64,128),0)<60,q,e)
    return q.astype(jnp.int32).astype(jnp.int16)

def kernel(x_any, fl, fc, nb_any, diag_any, coup_any, tri, outv,
           tab, stage, gt, ax, tt, sel, xo, xp, nb, idx, coup, diag, fbuf, fsend, ghost,
           loc, snd, rcv, psend,
           lsem, csem, xsem, fsem_s, fsem_r, qs, qr, ps, pr):
    ch=lax.axis_index("chaos"); m=lax.axis_index("mesh")
    y=ch//2; c=ch%2
    up=lax.rem(m+1,32); dn=lax.rem(m+31,32)
    peer={"chaos":2*y+1-c}; across={"chaos":2*(1-y)+c}
    near=[{"mesh":up,"chaos":ch},{"mesh":up,"chaos":2*y+1-c},{"mesh":dn,"chaos":ch},{"mesh":dn,"chaos":2*y+1-c}]
    half=pl.multiple_of(c*2048,2048)
    bar=pltpu.get_barrier_semaphore()
    for d in near+[peer,across]:
        pl.semaphore_signal(bar,inc=1,device_id=d,device_id_type=MESH)
    def lanes_of(t):
        return pl.ds(pl.multiple_of(half+t*128,128),128)
    def icopy(t,p):
        return pltpu.make_async_copy(nb.at[:,pl.ds(pl.multiple_of(t*128,128),128)],idx[p],lsem.at[1+p])
    loads=[pltpu.make_async_copy(coup_any.at[:,:,pl.ds(half,2048)],coup.at[e],csem.at[e]) for e in range(12)]
    loads.append(pltpu.make_async_copy(diag_any.at[:,pl.ds(half,2048)],diag,csem.at[12]))
    load=pltpu.make_async_copy(x_any,xo,lsem.at[0])
    load.start()
    nload=pltpu.make_async_copy(nb_any.at[:,pl.ds(half,2048)],nb,lsem.at[3])
    nload.start()
    for l in loads: l.start()
    load.wait(); nload.wait()
    nb[...]=nb[...]*2
    for p in range(2): icopy(p,p).start()
    build_table(xo,tab,0)
    gather_faces(fl,fc,tab,fbuf,fsend)
    prep_triple(tri,tt,y,c)
    r=iota((192,256),0); kk=iota((192,256),1)
    sel[...]=jnp.where(kk==jnp.where(r>=96,r+32,r),1.0,0.0).astype(BF)
    for p in range(2):
        gt[p][8]=jnp.zeros((192,128),F32)
        for cc in range(3): ax[p][cc]=jnp.zeros((576,256),BF)
    for p in range(2): icopy(p,p).wait()
    pl.semaphore_wait(bar,6)
    fcopies=[]
    for e,d in enumerate(near):
        side=1 if e<2 else 0
        f=pltpu.make_async_remote_copy(src_ref=fsend.at[side],dst_ref=ghost.at[e],send_sem=fsem_s.at[e],recv_sem=fsem_r.at[e],device_id=d,device_id_type=MESH)
        f.start(); fcopies.append(f)
    xcopy=pltpu.make_async_remote_copy(src_ref=xo,dst_ref=xp,send_sem=xsem.at[0],recv_sem=xsem.at[1],device_id=peer,device_id_type=MESH)
    xcopy.start()
    xcopy.wait()
    build_table(xp,tab,1)
    for f in fcopies: f.wait()
    low=jnp.where(m>0,1.0,0.0); high=jnp.where(m<31,1.0,0.0)
    for e in range(4):
        tab[pl.ds(8192+(e//2)*1024+e%2,512,stride=2),:]=ghost[e].astype(F32)*(low if e<2 else high)

    def qcopy(t):
        return pltpu.make_async_remote_copy(src_ref=snd.at[t+1],dst_ref=rcv.at[t+1],send_sem=qs.at[t+1],recv_sem=qr.at[t+1],device_id=across,device_id_type=MESH)
    def pcopy(t):
        lanes=pl.ds(pl.multiple_of(half+t*128,128),128)
        return pltpu.make_async_remote_copy(src_ref=psend.at[t],dst_ref=outv.at[:,:,lanes],send_sem=ps.at[t],recv_sem=pr.at[t],device_id=peer,device_id_type=MESH)
    def tmat(t,p,cs=(0,1,2)):
        for cc in cs:
            o=jnp.dot(tt[:,0:576],ax[p][cc],preferred_element_type=F32)
            o=o[:,0:128]+o[:,128:256]
            loc[t+1,cc]=o[0:64]
            snd[t+1,cc]=quantise(o[64:128])
    def finish(t):
        qcopy(t).wait()
        lanes=pl.ds(pl.multiple_of(half+t*128,128),128)
        for cc in range(3):
            v=rcv[t+1,cc].astype(jnp.int32).astype(F32)
            f=loc[t+1,cc]+v*jnp.exp2(v[60:61]*(1.0/64.0))
            outv[cc,:,lanes]=f[0:30]
            psend[t,cc]=f[30:60]
        pcopy(t).start()
    def gather_ops(p):
        return [functools.partial(gather_group,idx[p],tab,stage[p],g) for g in range(64)]
    def expand_ops(t,p):
        return ([functools.partial(expand_pair,sel,stage[p],gt[p],e) for e in range(4)]+
                [functools.partial(own_rows,(xo,xp),gt[p],lanes_of(t),h,cc) for h in range(2) for cc in range(3)])
    def body(t,p,gather=True,expand=True):
        at=pl.ds(pl.multiple_of(t*128,128),128)
        streams=[[functools.partial(combine,gt[p],coup.at[q*3+cc],diag,ax[p],at,q,cc,k) for q in range(4) for cc in range(3) for k in range(9)],
                 [functools.partial(tmat,t-1,1-p,(cc,)) for cc in range(3)]]
        if gather: streams.append(gather_ops(p))
        if expand: streams.append(expand_ops(t+1,1-p))
        interleave(streams)
    interleave([gather_ops(0)])
    interleave([gather_ops(1),expand_ops(0,0)])
    for p in range(2): icopy(p+2,p).start()
    for l in loads: l.wait()
    def pair(u,_):
        for p in range(2):
            icopy(2*u+2+p,p).wait()
            body(2*u+p,p)
            qcopy(2*u+p-1).start()
            icopy(jnp.minimum(2*u+4+p,NT-1),p).start()
        @pl.when(u>=LAG//2)
        def _():
            for p in range(2): finish(2*u-LAG+p)
        return 0
    lax.fori_loop(0,NT//2-1,pair,0)
    for p in range(2): icopy(NT-1,p).wait()
    body(NT-2,0,False,True)
    qcopy(NT-3).start()
    body(NT-1,1,False,False)
    qcopy(NT-2).start()
    tmat(NT-1,1)
    qcopy(NT-1).start()
    qcopy(-1).wait()
    for t in range(NT-2-LAG,NT): finish(t)
    for t in range(NT): pcopy(t).wait()

def call(x,fl,fc,nb,diag,coup,tri):
    V=pltpu.VMEM; D=pltpu.SemaphoreType.DMA; I16=jnp.int16
    anyspec=pl.BlockSpec(memory_space=pl.ANY); sm=pl.BlockSpec(memory_space=pltpu.SMEM); vm=pl.BlockSpec(memory_space=pltpu.VMEM)
    return pl.pallas_call(kernel,out_shape=pltpu.VMEM((3,30,4096),F32),
        in_specs=[anyspec,sm,sm,anyspec,anyspec,anyspec,vm],out_specs=vm,
        scratch_shapes=[V((10240,128),F32),[V((2048,128),F32)]*2,[V((9,192,128),F32)]*2,[V((3,576,256),BF)]*2,V((128,640),BF),V((192,256),BF),
            V((3,30,4096),BF),V((3,30,4096),BF),V((8,2048),jnp.int32),[pltpu.SMEM((8,128),jnp.int32)]*2,V((12,9,8,2048),F32),V((9,2048),F32),
            V((512,128),F32),V((2,512,128),BF),V((4,512,128),BF),
            V((NT+1,3,64,128),F32),V((NT+1,3,64,128),I16),V((NT+1,3,64,128),I16),V((NT,3,30,128),F32),
            D((4,)),D((13,)),D((2,)),D((4,)),D((4,)),D((NT+1,)),D((NT+1,)),D((NT,)),D((NT,))],
        compiler_params=pltpu.CompilerParams(vmem_limit_bytes=50<<20,collective_id=0,has_side_effects=True))(x,fl,fc,nb,diag,coup,tri)

def spread(v_ref, o_ref, sem):
    copy=pltpu.make_async_copy(v_ref,o_ref,sem)
    copy.start(); copy.wait()

def store(v):
    return pl.pallas_call(spread,out_shape=jax.ShapeDtypeStruct(v.shape,v.dtype),
        in_specs=[pl.BlockSpec(memory_space=pltpu.VMEM)],out_specs=pl.BlockSpec(memory_space=pl.ANY),
        scratch_shapes=[pltpu.SemaphoreType.DMA],compiler_params=pltpu.CompilerParams(vmem_limit_bytes=4<<20))(v)

def on_device(field_coeffs, face_list, face_count, neighbors, diag_modes, coupling, triple):
    x=jnp.transpose(field_coeffs,(1,0,2))
    out=store(call(x,face_list.reshape(8,128),face_count,neighbors,diag_modes,coupling,triple))
    return jnp.transpose(out,(1,0,2))

def solution(mesh):
    in_specs=(P("chaos",None,"mesh"),P("mesh",None,None),P("mesh",None),P(None,"mesh"),P(None,"mesh"),P(None,None,"mesh"),P())
    return jax.shard_map(on_device,mesh=mesh,in_specs=in_specs,out_specs=P("chaos",None,"mesh"),check_vma=False)
```

```python
import functools
import jax
import jax.numpy as jnp
from jax import lax
from jax.experimental import pallas as pl
from jax.experimental.pallas import tpu as pltpu
from jax.sharding import PartitionSpec as P
BF=jnp.bfloat16; F32=jnp.float32
NT=16
def iota(shape,d): return lax.broadcasted_iota(jnp.int32, shape, d)
def chaos_of(y,c,q):
    yy = jnp.where(q>=2, 1-y, y); cc = jnp.where(q%2==1, 1-c, c)
    return 2*yy+cc
def prep_triple(tri_ref, tt_ref, y, c):
    r=iota((128,120),0); i=iota((128,120),1)
    far=r>=64; w=jnp.where(far,r-64,r)
    other=w>=30; rr=jnp.where(other,w-30,w)
    d=2*jnp.where(far,1-y,y)+jnp.where(other,1-c,c)
    sel_l=jnp.where((rr<30)&(i==d*30+rr),1.0,0.0).astype(BF)
    j=iota((120,128),0); a=iota((120,128),1)
    for k in range(9):
        tl=jnp.dot(sel_l,tri_ref[k],preferred_element_type=F32).astype(BF)
        off=64*(k%2)
        b=a-off; h=b//32; bb=b%32
        dj=2*y+jnp.where(h==1,1-c,c)
        sel_r=jnp.where((b>=0)&(b<64)&(bb<30)&(j==dj*30+bb),1.0,0.0).astype(BF)
        t=jnp.dot(tl,sel_r,preferred_element_type=F32)
        if k%2==0: keep=t
        if k%2==1: tt_ref[:, (k-1)*64:(k+1)*64]=(keep+t).astype(BF)
    tt_ref[:, 512:640]=keep.astype(BF)
def gather_group(idx, tab, stage, g):
    s,u0=g//8,(g%8)*16
    vs=[tab[pl.ds(idx[s,u0+u],2),:] for u in range(16)]
    for u in range(16):
        stage[pl.ds((s*128+u0+u)*2,2),:]=vs[u]

def expand_pair(sel_ref, stage, gt, p):
    rows=[jnp.concatenate([stage[pl.ds(s*256+h,128,stride=2),:] for h in range(2)],axis=1).astype(BF) for s in (2*p,2*p+1)]
    r=lax.dot_general(sel_ref[...],jnp.concatenate(rows,axis=0),(((1,),(1,)),((),())),preferred_element_type=F32)
    for e in range(2): gt[2*p+e]=r[:,e*128:(e+1)*128]

def own_rows(xs, gt, lanes, h, cc):
    gt[8,h*96+cc*32:h*96+cc*32+30,:]=xs[h][cc,:,lanes].astype(F32)

def combine(gt, coup, diag, ax, at, q, cc, k):
    h,jh=q//2,q%2
    r0=h*96+cc*32+jh*16
    acc=diag[k:k+1,at]*gt[8,r0:r0+16,:]
    for s in range(8):
        acc=acc-coup[k,s:s+1,at]*gt[s,r0:r0+16,:]
    hi=acc.astype(BF)
    lo=(acc-hi.astype(F32)).astype(BF)
    ro=k*64+h*32+jh*16
    ax[cc,ro:ro+16,0:128]=hi
    ax[cc,ro:ro+16,128:256]=lo

def interleave(streams):
    ops=[]
    for n,st in enumerate(streams):
        for e,f in enumerate(st): ops.append(((e+0.5)/len(st),n,f))
    for _,_,f in sorted(ops,key=lambda o:o[:2]): f()

MESH=pl.DeviceIdType.MESH
LAG=6

def build_table(x, tab, h):
    def block(b):
        lanes=pl.ds(pl.multiple_of(b*128,128),128)
        z2=jnp.zeros((2,128),F32)
        parts=[]
        for cc in range(3):
            parts += [x[cc,:,lanes].astype(F32), z2]
        parts.append(jnp.zeros((32,128),F32))
        return jnp.concatenate(parts,axis=0).T
    def body(b,_):
        vs=[block(4*b+e) for e in range(4)]
        for e in range(4): tab[pl.ds(256*(4*b+e)+h,128,stride=2),:]=vs[e]
        return 0
    lax.fori_loop(0,8,body,0)

def gather_faces(fl, fc, tab, fbuf, fsend):
    for side in range(2):
        for b in range(32):
            vs=[tab[pl.ds(fl[0,side,b*16+u]*2,1),:] for u in range(16)]
            for u in range(16): fbuf[pl.ds(b*16+u,1),:]=vs[u]
        keep=iota((512,128),0)<fc[0,side]
        fsend[side]=jnp.where(keep,fbuf[...],0.0).astype(BF)

def quantise(o):
    top=jnp.maximum(jnp.max(jnp.abs(o),axis=0,keepdims=True),1e-30)
    e=jnp.ceil(64.0*jnp.log2(top*(1.0/32760.0)))
    q=jnp.clip(jnp.round(o*jnp.exp2(e*(-1.0/64.0))),-32767.0,32767.0)
    q=jnp.where(iota((64,128),0)<60,q,e)
    return q.astype(jnp.int32).astype(jnp.int16)

def kernel(x_any, fl_any, fc_any, nb_any, diag_any, coup_any, tri_any, outv,
           tab, stage, gt, ax, tt, sel, xo, xp, fl, fc, tri, nb, idx, coup, diag, fbuf, fsend, ghost,
           loc, snd, rcv, psend,
           lsem, csem, xsem, fsem_s, fsem_r, qs, qr, ps, pr):
    ch=lax.axis_index("chaos"); m=lax.axis_index("mesh")
    y=ch//2; c=ch%2
    up=lax.rem(m+1,32); dn=lax.rem(m+31,32)
    peer={"chaos":2*y+1-c}; across={"chaos":2*(1-y)+c}
    near=[{"mesh":up,"chaos":ch},{"mesh":up,"chaos":2*y+1-c},{"mesh":dn,"chaos":ch},{"mesh":dn,"chaos":2*y+1-c}]
    half=pl.multiple_of(c*2048,2048)
    bar=pltpu.get_barrier_semaphore()
    for d in near+[peer,across]:
        pl.semaphore_signal(bar,inc=1,device_id=d,device_id_type=MESH)
    def lanes_of(t):
        return pl.ds(pl.multiple_of(half+t*128,128),128)
    def icopy(t,p):
        return pltpu.make_async_copy(nb.at[:,pl.ds(pl.multiple_of(t*128,128),128)],idx[p],lsem.at[1+p])
    loads=[pltpu.make_async_copy(coup_any.at[:,:,pl.ds(half,2048)],coup.at[e],csem.at[e]) for e in range(12)]
    loads.append(pltpu.make_async_copy(diag_any.at[:,pl.ds(half,2048)],diag,csem.at[12]))
    load=pltpu.make_async_copy(x_any,xo,lsem.at[0])
    load.start()
    nload=pltpu.make_async_copy(nb_any.at[:,pl.ds(half,2048)],nb,lsem.at[3])
    nload.start()
    small=[pltpu.make_async_copy(a,b,lsem.at[4+e]) for e,(a,b) in enumerate(((fl_any,fl),(fc_any,fc),(tri_any,tri)))]
    for l in small: l.start()
    load.wait()
    pl.semaphore_wait(bar,6)
    xcopy=pltpu.make_async_remote_copy(src_ref=xo,dst_ref=xp,send_sem=xsem.at[0],recv_sem=xsem.at[1],device_id=peer,device_id_type=MESH)
    xcopy.start()
    nload.wait()
    nb[...]=nb[...]*2
    for l in small: l.wait()
    for p in range(2): icopy(p,p).start()
    build_table(xo,tab,0)
    gather_faces(fl,fc,tab,fbuf,fsend)
    for p in range(2): icopy(p,p).wait()
    fcopies=[]
    for e,d in enumerate(near):
        side=1 if e<2 else 0
        f=pltpu.make_async_remote_copy(src_ref=fsend.at[side],dst_ref=ghost.at[e],send_sem=fsem_s.at[e],recv_sem=fsem_r.at[e],device_id=d,device_id_type=MESH)
        f.start(); fcopies.append(f)
    prep_triple(tri,tt,y,c)
    r=iota((192,256),0); kk=iota((192,256),1)
    sel[...]=jnp.where(kk==jnp.where(r>=96,r+32,r),1.0,0.0).astype(BF)
    for p in range(2):
        gt[p][8]=jnp.zeros((192,128),F32)
        for cc in range(3): ax[p][cc]=jnp.zeros((576,256),BF)
    xcopy.wait()
    for l in loads: l.start()
    build_table(xp,tab,1)
    for f in fcopies: f.wait()
    low=jnp.where(m>0,1.0,0.0); high=jnp.where(m<31,1.0,0.0)
    for e in range(4):
        tab[pl.ds(8192+(e//2)*1024+e%2,512,stride=2),:]=ghost[e].astype(F32)*(low if e<2 else high)

    def qcopy(t):
        return pltpu.make_async_remote_copy(src_ref=snd.at[t+1],dst_ref=rcv.at[t+1],send_sem=qs.at[t+1],recv_sem=qr.at[t+1],device_id=across,device_id_type=MESH)
    def pcopy(t):
        lanes=pl.ds(pl.multiple_of(half+t*128,128),128)
        return pltpu.make_async_remote_copy(src_ref=psend.at[t],dst_ref=outv.at[:,:,lanes],send_sem=ps.at[t],recv_sem=pr.at[t],device_id=peer,device_id_type=MESH)
    def tmat(t,p,cs=(0,1,2)):
        for cc in cs:
            o=jnp.dot(tt[:,0:576],ax[p][cc],preferred_element_type=F32)
            o=o[:,0:128]+o[:,128:256]
            loc[t+1,cc]=o[0:64]
            snd[t+1,cc]=quantise(o[64:128])
    def finish(t):
        qcopy(t).wait()
        lanes=pl.ds(pl.multiple_of(half+t*128,128),128)
        for cc in range(3):
            v=rcv[t+1,cc].astype(jnp.int32).astype(F32)
            f=loc[t+1,cc]+v*jnp.exp2(v[60:61]*(1.0/64.0))
            outv[cc,:,lanes]=f[0:30]
            psend[t,cc]=f[30:60]
        pcopy(t).start()
    def gather_ops(p):
        return [functools.partial(gather_group,idx[p],tab,stage[p],g) for g in range(64)]
    def expand_ops(t,p):
        return ([functools.partial(expand_pair,sel,stage[p],gt[p],e) for e in range(4)]+
                [functools.partial(own_rows,(xo,xp),gt[p],lanes_of(t),h,cc) for h in range(2) for cc in range(3)])
    def body(t,p,gather=True,expand=True):
        at=pl.ds(pl.multiple_of(t*128,128),128)
        streams=[[functools.partial(combine,gt[p],coup.at[q*3+cc],diag,ax[p],at,q,cc,k) for q in range(4) for cc in range(3) for k in range(9)],
                 [functools.partial(tmat,t-1,1-p,(cc,)) for cc in range(3)]]
        if gather: streams.append(gather_ops(p))
        if expand: streams.append(expand_ops(t+1,1-p))
        interleave(streams)
    interleave([gather_ops(0)])
    interleave([gather_ops(1),expand_ops(0,0)])
    for p in range(2): icopy(p+2,p).start()
    for l in loads: l.wait()
    def pair(u,_):
        for p in range(2):
            icopy(2*u+2+p,p).wait()
            body(2*u+p,p)
            if p:
                qcopy(2*u).start()
            else:
                @pl.when(u>0)
                def _(): qcopy(2*u-1).start()
            icopy(jnp.minimum(2*u+4+p,NT-1),p).start()
        @pl.when(u>=LAG//2)
        def _():
            for p in range(2): finish(2*u-LAG+p)
        return 0
    lax.fori_loop(0,NT//2-1,pair,0)
    for p in range(2): icopy(NT-1,p).wait()
    body(NT-2,0,False,True)
    qcopy(NT-3).start()
    body(NT-1,1,False,False)
    qcopy(NT-2).start()
    tmat(NT-1,1)
    qcopy(NT-1).start()
    for t in range(NT-2-LAG,NT): finish(t)
    for t in range(NT): pcopy(t).wait()

def call(x,fl,fc,nb,diag,coup,tri):
    V=pltpu.VMEM; D=pltpu.SemaphoreType.DMA; I16=jnp.int16
    anyspec=pl.BlockSpec(memory_space=pl.ANY); vm=pl.BlockSpec(memory_space=pltpu.VMEM)
    return pl.pallas_call(kernel,out_shape=pltpu.VMEM((3,30,4096),F32),
        in_specs=[anyspec]*7,out_specs=vm,
        scratch_shapes=[V((10240,128),F32),[V((2048,128),F32)]*2,[V((9,192,128),F32)]*2,[V((3,576,256),BF)]*2,V((128,640),BF),V((192,256),BF),
            V((3,30,4096),BF),V((3,30,4096),BF),pltpu.SMEM((1,2,512),jnp.int32),pltpu.SMEM((1,2),jnp.int32),V((9,120,120),BF),V((8,2048),jnp.int32),[pltpu.SMEM((8,128),jnp.int32)]*2,V((12,9,8,2048),F32),V((9,2048),F32),
            V((512,128),F32),V((2,512,128),BF),V((4,512,128),BF),
            V((NT+1,3,64,128),F32),V((NT+1,3,64,128),I16),V((NT+1,3,64,128),I16),V((NT,3,30,128),F32),
            D((7,)),D((13,)),D((2,)),D((4,)),D((4,)),D((NT+1,)),D((NT+1,)),D((NT,)),D((NT,))],
        compiler_params=pltpu.CompilerParams(vmem_limit_bytes=61<<20,collective_id=0,has_side_effects=True))(x,fl,fc,nb,diag,coup,tri)

def spread(v_ref, o_ref, sem):
    copy=pltpu.make_async_copy(v_ref,o_ref,sem)
    copy.start(); copy.wait()

def store(v):
    return pl.pallas_call(spread,out_shape=jax.ShapeDtypeStruct(v.shape,v.dtype),
        in_specs=[pl.BlockSpec(memory_space=pltpu.VMEM)],out_specs=pl.BlockSpec(memory_space=pl.ANY),
        scratch_shapes=[pltpu.SemaphoreType.DMA],compiler_params=pltpu.CompilerParams(vmem_limit_bytes=4<<20))(v)

def on_device(field_coeffs, face_list, face_count, neighbors, diag_modes, coupling, triple):
    x=jnp.transpose(field_coeffs,(1,0,2))
    out=store(call(x,face_list,face_count,neighbors,diag_modes,coupling,triple))
    return jnp.transpose(out,(1,0,2))

def solution(mesh):
    in_specs=(P("chaos",None,"mesh"),P("mesh",None,None),P("mesh",None),P(None,"mesh"),P(None,"mesh"),P(None,None,"mesh"),P())
    return jax.shard_map(on_device,mesh=mesh,in_specs=in_specs,out_specs=P("chaos",None,"mesh"),check_vma=False)
```

```python
import functools
import jax
import jax.numpy as jnp
from jax import lax
from jax.experimental import pallas as pl
from jax.experimental.pallas import tpu as pltpu
from jax.sharding import PartitionSpec as P
BF=jnp.bfloat16; F32=jnp.float32
NT=16
def iota(shape,d): return lax.broadcasted_iota(jnp.int32, shape, d)
def chaos_of(y,c,q):
    yy = jnp.where(q>=2, 1-y, y); cc = jnp.where(q%2==1, 1-c, c)
    return 2*yy+cc
def prep_triple(tri_ref, tt_ref, y, c):
    r=iota((128,120),0); i=iota((128,120),1)
    far=r>=64; w=jnp.where(far,r-64,r)
    other=w>=30; rr=jnp.where(other,w-30,w)
    d=2*jnp.where(far,1-y,y)+jnp.where(other,1-c,c)
    sel_l=jnp.where((rr<30)&(i==d*30+rr),1.0,0.0).astype(BF)
    j=iota((120,128),0); a=iota((120,128),1)
    for k in range(9):
        tl=jnp.dot(sel_l,tri_ref[k],preferred_element_type=F32).astype(BF)
        off=64*(k%2)
        b=a-off; h=b//32; bb=b%32
        dj=2*y+jnp.where(h==1,1-c,c)
        sel_r=jnp.where((b>=0)&(b<64)&(bb<30)&(j==dj*30+bb),1.0,0.0).astype(BF)
        t=jnp.dot(tl,sel_r,preferred_element_type=F32)
        if k%2==0: keep=t
        if k%2==1: tt_ref[:, (k-1)*64:(k+1)*64]=(keep+t).astype(BF)
    tt_ref[:, 512:640]=keep.astype(BF)
def gather_group(idx, tab, stage, g):
    s,u0=g//8,(g%8)*16
    vs=[tab[pl.ds(idx[s,u0+u],2),:] for u in range(16)]
    for u in range(16):
        stage[pl.ds((s*128+u0+u)*2,2),:]=vs[u]

def expand_part(stage, gt, p):
    s,h=p//2,p%2
    gt[s,h*96:(h+1)*96,:]=stage[pl.ds(s*256+h,128,stride=2),:].astype(BF).T[0:96].astype(F32)

def own_rows(xs, gt, lanes, h, cc):
    gt[8,h*96+cc*32:h*96+cc*32+30,:]=xs[h][cc,:,lanes].astype(F32)

def combine(gt, coup, diag, ax, at, q, cc, k):
    h,jh=q//2,q%2
    r0=h*96+cc*32+jh*16
    acc=diag[k:k+1,at]*gt[8,r0:r0+16,:]
    for s in range(8):
        acc=acc-coup[k,s:s+1,at]*gt[s,r0:r0+16,:]
    hi=acc.astype(BF)
    lo=(acc-hi.astype(F32)).astype(BF)
    ro=k*64+h*32+jh*16
    ax[cc,ro:ro+16,0:128]=hi
    ax[cc,ro:ro+16,128:256]=lo

def interleave(streams):
    ops=[]
    for n,st in enumerate(streams):
        for e,f in enumerate(st): ops.append(((e+0.5)/len(st),n,f))
    for _,_,f in sorted(ops,key=lambda o:o[:2]): f()

MESH=pl.DeviceIdType.MESH
LAG=6

def build_table(x, tab, h):
    def block(b):
        lanes=pl.ds(pl.multiple_of(b*128,128),128)
        z2=jnp.zeros((2,128),F32)
        parts=[]
        for cc in range(3):
            parts += [x[cc,:,lanes].astype(F32), z2]
        parts.append(jnp.zeros((32,128),F32))
        return jnp.concatenate(parts,axis=0).T
    def body(b,_):
        vs=[block(4*b+e) for e in range(4)]
        for e in range(4): tab[pl.ds(256*(4*b+e)+h,128,stride=2),:]=vs[e]
        return 0
    lax.fori_loop(0,8,body,0)

def gather_faces(fl, fc, tab, fbuf, fsend):
    for side in range(2):
        for b in range(32):
            vs=[tab[pl.ds(fl[0,side,b*16+u],1),:] for u in range(16)]
            for u in range(16): fbuf[pl.ds(b*16+u,1),:]=vs[u]
        keep=iota((512,128),0)<fc[0,side]
        fsend[side]=jnp.where(keep,fbuf[...],0.0).astype(BF)

def quantise(o):
    top=jnp.maximum(jnp.max(jnp.abs(o),axis=0,keepdims=True),1e-30)
    e=jnp.ceil(64.0*jnp.log2(top*(1.0/32760.0)))
    q=jnp.clip(jnp.round(o*jnp.exp2(e*(-1.0/64.0))),-32767.0,32767.0)
    q=jnp.where(iota((64,128),0)<60,q,e)
    return q.astype(jnp.int32).astype(jnp.int16)

def kernel(x_any, fl_any, fc_any, nb_any, diag_any, coup_any, tri_any, outv,
           tab, stage, gt, ax, tt, xo, xp, fv, fl, fc, tri, nb, idx, coup, diag, fbuf, fsend, ghost,
           loc, snd, rcv, psend,
           lsem, csem, xsem, fsem_s, fsem_r, qs, qr, ps, pr):
    ch=lax.axis_index("chaos"); m=lax.axis_index("mesh")
    y=ch//2; c=ch%2
    up=lax.rem(m+1,32); dn=lax.rem(m+31,32)
    peer={"chaos":2*y+1-c}; across={"chaos":2*(1-y)+c}
    near=[{"mesh":up,"chaos":ch},{"mesh":up,"chaos":2*y+1-c},{"mesh":dn,"chaos":ch},{"mesh":dn,"chaos":2*y+1-c}]
    half=pl.multiple_of(c*2048,2048)
    bar=pltpu.get_barrier_semaphore()
    for d in near+[peer,across]:
        pl.semaphore_signal(bar,inc=1,device_id=d,device_id_type=MESH)
    def lanes_of(t):
        return pl.ds(pl.multiple_of(half+t*128,128),128)
    def icopy(t,p):
        return pltpu.make_async_copy(nb.at[:,pl.ds(pl.multiple_of(t*128,128),128)],idx[p],lsem.at[1+p])
    loads=[pltpu.make_async_copy(coup_any.at[:,:,pl.ds(half,2048)],coup.at[e],csem.at[e]) for e in range(12)]
    loads.append(pltpu.make_async_copy(diag_any.at[:,pl.ds(half,2048)],diag,csem.at[12]))
    load=pltpu.make_async_copy(x_any,xo,lsem.at[0])
    load.start()
    nload=pltpu.make_async_copy(nb_any.at[:,pl.ds(half,2048)],nb,lsem.at[3])
    nload.start()
    small=[pltpu.make_async_copy(a,b,lsem.at[4+e]) for e,(a,b) in enumerate(((fl_any,fv),(fc_any,fc),(tri_any,tri)))]
    for l in small: l.start()
    for l in small: l.wait()
    fv[...]=fv[...]*2
    flcopy=pltpu.make_async_copy(fv,fl,lsem.at[4])
    flcopy.start()
    load.wait()
    pl.semaphore_wait(bar,6)
    xcopy=pltpu.make_async_remote_copy(src_ref=xo,dst_ref=xp,send_sem=xsem.at[0],recv_sem=xsem.at[1],device_id=peer,device_id_type=MESH)
    xcopy.start()
    nload.wait()
    nb[...]=nb[...]*2
    for p in range(2): icopy(p,p).start()
    build_table(xo,tab,0)
    flcopy.wait()
    gather_faces(fl,fc,tab,fbuf,fsend)
    fcopies=[]
    for e,d in enumerate(near):
        side=1 if e<2 else 0
        f=pltpu.make_async_remote_copy(src_ref=fsend.at[side],dst_ref=ghost.at[e],send_sem=fsem_s.at[e],recv_sem=fsem_r.at[e],device_id=d,device_id_type=MESH)
        f.start(); fcopies.append(f)
    prep_triple(tri,tt,y,c)
    for p in range(2):
        gt[p][8]=jnp.zeros((192,128),F32)
        for cc in range(3): ax[p][cc]=jnp.zeros((576,256),BF)
    xcopy.wait()
    for l in loads: l.start()
    for p in range(2): icopy(p,p).wait()
    build_table(xp,tab,1)
    for f in fcopies: f.wait()
    low=jnp.where(m>0,1.0,0.0); high=jnp.where(m<31,1.0,0.0)
    for e in range(4):
        tab[pl.ds(8192+(e//2)*1024+e%2,512,stride=2),:]=ghost[e].astype(F32)*(low if e<2 else high)

    def qcopy(t):
        return pltpu.make_async_remote_copy(src_ref=snd.at[t+1],dst_ref=rcv.at[t+1],send_sem=qs.at[t+1],recv_sem=qr.at[t+1],device_id=across,device_id_type=MESH)
    def pcopy(t):
        lanes=pl.ds(pl.multiple_of(half+t*128,128),128)
        return pltpu.make_async_remote_copy(src_ref=psend.at[t],dst_ref=outv.at[:,:,lanes],send_sem=ps.at[t],recv_sem=pr.at[t],device_id=peer,device_id_type=MESH)
    def tmat(t,p,cs=(0,1,2)):
        for cc in cs:
            o=jnp.dot(tt[:,0:576],ax[p][cc],preferred_element_type=F32)
            o=o[:,0:128]+o[:,128:256]
            loc[t+1,cc]=o[0:64]
            snd[t+1,cc]=quantise(o[64:128])
    def finish(t):
        qcopy(t).wait()
        lanes=pl.ds(pl.multiple_of(half+t*128,128),128)
        for cc in range(3):
            v=rcv[t+1,cc].astype(jnp.int32).astype(F32)
            f=loc[t+1,cc]+v*jnp.exp2(v[60:61]*(1.0/64.0))
            outv[cc,:,lanes]=f[0:30]
            psend[t,cc]=f[30:60]
        pcopy(t).start()
    def gather_ops(p):
        return [functools.partial(gather_group,idx[p],tab,stage[p],g) for g in range(64)]
    def expand_ops(t,p):
        return ([functools.partial(expand_part,stage[p],gt[p],e) for e in range(16)]+
                [functools.partial(own_rows,(xo,xp),gt[p],lanes_of(t),h,cc) for h in range(2) for cc in range(3)])
    def body(t,p,gather=True,expand=True):
        at=pl.ds(pl.multiple_of(t*128,128),128)
        streams=[[functools.partial(combine,gt[p],coup.at[q*3+cc],diag,ax[p],at,q,cc,k) for q in range(4) for cc in range(3) for k in range(9)],
                 [functools.partial(tmat,t-1,1-p,(cc,)) for cc in range(3)]]
        if gather: streams.append(gather_ops(p))
        if expand: streams.append(expand_ops(t+1,1-p))
        interleave(streams)
    interleave([gather_ops(0)])
    interleave([gather_ops(1),expand_ops(0,0)])
    for p in range(2): icopy(p+2,p).start()
    for l in loads: l.wait()
    def pair(u,_):
        for p in range(2):
            icopy(2*u+2+p,p).wait()
            body(2*u+p,p)
            if p:
                qcopy(2*u).start()
            else:
                @pl.when(u>0)
                def _(): qcopy(2*u-1).start()
            icopy(jnp.minimum(2*u+4+p,NT-1),p).start()
        @pl.when(u>=LAG//2)
        def _():
            for p in range(2): finish(2*u-LAG+p)
        return 0
    lax.fori_loop(0,NT//2-1,pair,0)
    for p in range(2): icopy(NT-1,p).wait()
    body(NT-2,0,False,True)
    qcopy(NT-3).start()
    body(NT-1,1,False,False)
    qcopy(NT-2).start()
    tmat(NT-1,1)
    qcopy(NT-1).start()
    for t in range(NT-2-LAG,NT): finish(t)
    for t in range(NT): pcopy(t).wait()

def call(x,fl,fc,nb,diag,coup,tri):
    V=pltpu.VMEM; D=pltpu.SemaphoreType.DMA; I16=jnp.int16
    anyspec=pl.BlockSpec(memory_space=pl.ANY); vm=pl.BlockSpec(memory_space=pltpu.VMEM)
    return pl.pallas_call(kernel,out_shape=pltpu.VMEM((3,30,4096),F32),
        in_specs=[anyspec]*7,out_specs=vm,
        scratch_shapes=[V((10240,128),F32),[V((2048,128),F32)]*2,[V((9,192,128),F32)]*2,[V((3,576,256),BF)]*2,V((128,640),BF),
            V((3,30,4096),BF),V((3,30,4096),BF),V((1,2,512),jnp.int32),pltpu.SMEM((1,2,512),jnp.int32),pltpu.SMEM((1,2),jnp.int32),V((9,120,120),BF),V((8,2048),jnp.int32),[pltpu.SMEM((8,128),jnp.int32)]*2,V((12,9,8,2048),F32),V((9,2048),F32),
            V((512,128),F32),V((2,512,128),BF),V((4,512,128),BF),
            V((NT+1,3,64,128),F32),V((NT+1,3,64,128),I16),V((NT+1,3,64,128),I16),V((NT,3,30,128),F32),
            D((7,)),D((13,)),D((2,)),D((4,)),D((4,)),D((NT+1,)),D((NT+1,)),D((NT,)),D((NT,))],
        compiler_params=pltpu.CompilerParams(vmem_limit_bytes=61<<20,collective_id=0,has_side_effects=True))(x,fl,fc,nb,diag,coup,tri)

def spread(v_ref, o_ref, sem):
    copy=pltpu.make_async_copy(v_ref,o_ref,sem)
    copy.start(); copy.wait()

def store(v):
    return pl.pallas_call(spread,out_shape=jax.ShapeDtypeStruct(v.shape,v.dtype),
        in_specs=[pl.BlockSpec(memory_space=pltpu.VMEM)],out_specs=pl.BlockSpec(memory_space=pl.ANY),
        scratch_shapes=[pltpu.SemaphoreType.DMA],compiler_params=pltpu.CompilerParams(vmem_limit_bytes=4<<20))(v)

def on_device(field_coeffs, face_list, face_count, neighbors, diag_modes, coupling, triple):
    x=jnp.transpose(field_coeffs,(1,0,2))
    out=store(call(x,face_list,face_count,neighbors,diag_modes,coupling,triple))
    return jnp.transpose(out,(1,0,2))

def solution(mesh):
    in_specs=(P("chaos",None,"mesh"),P("mesh",None,None),P("mesh",None),P(None,"mesh"),P(None,"mesh"),P(None,None,"mesh"),P())
    return jax.shard_map(on_device,mesh=mesh,in_specs=in_specs,out_specs=P("chaos",None,"mesh"),check_vma=False)
```
